32 devices in a mesh: replica: 4 (over z), fsdp: 2 (over y), tensor: 4 (over x, core).
Axes of the slice: x: 2, y: 2, z: 4, core: 2. Of those that a mesh axis runs over, the one named last changes fastest.
Arguments:
- activations: bfloat16 [1024, 8192], P(('replica', 'fsdp')), may hold values from -6 to 6
- value_grads: bfloat16 [1024, 2048], P(('replica', 'fsdp'), 'tensor'), may hold values from -6 to 6
- lengths: int32 [16], P(('replica', 'fsdp')), may hold values from 16 to 64, as said below
- master: float32 [8192, 2048], P('fsdp', 'tensor'), may hold values from -0.0625 to 0.0625
- moment_one: float32 [8192, 2048], P('fsdp', 'tensor'), may hold values from -0.078125 to 0.078125
- moment_two: float32 [8192, 2048], P('fsdp', 'tensor'), may hold values from 1e-06 to 0.0001
Outputs:
- input_grads: bfloat16 [1024, 8192], P(('replica', 'fsdp'), 'tensor')
- new_master: float32 [8192, 2048], P('fsdp', 'tensor')
- new_moment_one: float32 [8192, 2048], P('fsdp', 'tensor')
- new_moment_two: float32 [8192, 2048], P('fsdp', 'tensor')
The draws below stay inside these ranges and needn't reach their ends.
Inputs may be any that keep to these rules, and one draw needn't show every extreme that they name: `lengths`: each sequence's live tokens form a prefix of its 64 positions.
All inputs are finite; a program needn't handle non-finite values.
Results may differ from the reference program's by a relative error of at most 0.014.
Values may be sent and summed in bfloat16 or wider, within the bound.
A program may use at most 128 MiB of HBM per device.

```python
import math
import jax
import jax.numpy as jnp
from jax import lax

D = 8192
SEQ = 64
KV = 2048
TOK_DEV = 128
SEQS = 16
TOKENS = 1024
N_REPLICA = 4
N_FSDP = 2
N_TENSOR = 4


def draw_lengths(key, part):
    values = jax.random.randint(key, (SEQS,), SEQ // 4, SEQ + 1, dtype=jnp.int32)
    return values.at[0].set(SEQ)


def shard_levels(own_key, extent, split, least, high):
    def one(dim, parts):
        steps = jax.random.uniform(jax.random.fold_in(jax.random.fold_in(own_key, 6), dim), (parts,), jnp.float32, least / len(split), high / len(split))
        return jnp.repeat(jnp.exp(steps), extent[dim] // parts).reshape((-1,) + (1,) * (len(extent) - dim - 1))

    level = one(*split[0])
    for cut in split[1:]:
        level = level * one(*cut)
    return level


def noise(rng, shape, spread, reach, split=(), held_as=jnp.bfloat16):
    gain = shard_levels(rng, shape, split, -0.22, 0.18) if split else 1.0
    result = jax.random.normal(rng, shape, jnp.float32) * spread * gain
    return jnp.minimum(jnp.maximum(result, -reach), reach).astype(held_as)


def setup_inputs(seed: int = 0) -> dict:
    key_list = jax.random.split(jax.random.key(seed), 7)
    activations = noise(key_list[0], (TOKENS, D), 1.0, 6.0, ((0, 8),))
    value_grads = noise(key_list[1], (TOKENS, KV), 1.0, 6.0, ((0, 8), (1, 4)))
    lengths = draw_lengths(jax.random.fold_in(key_list[6], 71), 0)
    master = noise(key_list[3], (D, KV), D ** -0.5, 0.0625, ((0, 2), (1, 4)), jnp.float32)
    moment_one = noise(key_list[4], (D, KV), 0.005, 0.078125, ((0, 2), (1, 4)), jnp.float32)
    moment_two = jnp.clip(jnp.exp(math.log(0.0001) - 4.6051702 * jax.random.uniform(key_list[5], (D, KV), jnp.float32) ** shard_levels(key_list[5], (D, KV), ((0, 2), (1, 4)), -0.2, 0.2)), 9.999999974752427e-07, 0.0001)
    return dict(activations=activations, value_grads=value_grads, lengths=lengths, master=master, moment_one=moment_one, moment_two=moment_two)


beta_one = 0.9
beta_two = 0.95
learn_rate = 0.001
weight_decay = 0.1
adam_step = 10
epsilon = 1e-08

def adamw(grad, master, moment_one, moment_two):
    first = beta_one * moment_one + (1.0 - beta_one) * grad
    second = beta_two * moment_two + (1.0 - beta_two) * grad * grad
    first_hat = first / (1.0 - beta_one ** adam_step)
    second_hat = second / (1.0 - beta_two ** adam_step)
    updated = master - learn_rate * (first_hat / (jnp.sqrt(second_hat) + epsilon) + weight_decay * master)
    return (updated, first, second)

def reference(activations, value_grads, lengths, master, moment_one, moment_two):
    total_tokens = activations.shape[0]
    width = activations.shape[1]
    columns = value_grads.shape[1]
    index = jnp.arange(total_tokens, dtype=jnp.int32)
    limit = lengths[index // SEQ]
    masked = jnp.where((index % SEQ < limit)[:, None], value_grads, jnp.zeros_like(value_grads))
    weight = master.astype(jnp.bfloat16)
    block = columns // N_TENSOR
    summed = jnp.zeros((total_tokens, width), jnp.float32)
    for head_block in range(N_TENSOR):
        part = jnp.dot(masked[:, head_block * block:(head_block + 1) * block], weight[:, head_block * block:(head_block + 1) * block].T, preferred_element_type=jnp.float32)
        part = lax.optimization_barrier(part.astype(jnp.bfloat16))
        summed = summed + part.astype(jnp.float32)
    input_grads = summed.astype(jnp.bfloat16)
    ranks = N_REPLICA * N_FSDP
    act_blocks = activations.reshape(ranks, TOK_DEV, width)
    grad_blocks = masked.reshape(ranks, TOK_DEV, columns)

    def accumulate(carry, pair):
        term = lax.dot_general(pair[0], pair[1], (((0,), (0,)), ((), ())), preferred_element_type=jnp.float32)
        term = lax.optimization_barrier(term.astype(jnp.bfloat16))
        return (carry + term.astype(jnp.float32), None)
    grad_sum, _ = lax.scan(accumulate, jnp.zeros((width, columns), jnp.float32), (act_blocks, grad_blocks))
    grad = grad_sum / float(total_tokens)
    new_master, new_one, new_two = adamw(grad, master, moment_one, moment_two)
    return (input_grads, new_master, new_one, new_two)
```

```python
import functools

import jax
import jax.numpy as jnp
from jax import lax
from jax.experimental import pallas as pl
from jax.experimental.pallas import tpu as pltpu
from jax.sharding import PartitionSpec as P

MESH = pl.DeviceIdType.MESH
LANE = 128

beta_one = 0.9
beta_two = 0.95
learn_rate = 0.001
weight_decay = 0.1
adam_step = 10
epsilon = 1e-08


def adamw(grad, master, moment_one, moment_two):
    first = beta_one * moment_one + (1.0 - beta_one) * grad
    second = beta_two * moment_two + (1.0 - beta_two) * grad * grad
    first_hat = first / (1.0 - beta_one**adam_step)
    second_hat = second / (1.0 - beta_two**adam_step)
    updated = master - learn_rate * (
        first_hat / (jnp.sqrt(second_hat) + epsilon) + weight_decay * master
    )
    return (updated, first, second)


def local(activations, value_grads, lengths, master, moment_one, moment_two):
    tok_rows = activations.shape[0]
    seq_count = lengths.shape[0]
    seq_len = tok_rows // seq_count
    index = jnp.arange(tok_rows, dtype=jnp.int32)
    owner = index // seq_len
    pick = owner[:, None] == jnp.arange(seq_count, dtype=jnp.int32)[None, :]
    limit = jnp.sum(jnp.where(pick, lengths[None, :], 0), axis=1)
    masked = jnp.where((index % seq_len < limit)[:, None], value_grads, jnp.zeros_like(value_grads))
    weight = master.astype(jnp.bfloat16)
    terms = lax.dot_general(
        masked,
        lax.all_gather(weight, "fsdp", axis=0, tiled=True),
        (((1,), (1,)), ((), ())),
        preferred_element_type=jnp.float32,
    )
    input_grads = lax.psum_scatter(
        terms.astype(jnp.bfloat16), "tensor", scatter_dimension=1, tiled=True
    )
    shard_rows = lax.psum_scatter(
        lax.dot_general(
            activations, masked, (((0,), (0,)), ((), ())), preferred_element_type=jnp.float32
        ).astype(jnp.bfloat16),
        "fsdp",
        scatter_dimension=0,
        tiled=True,
    )
    count = float(tok_rows * lax.axis_size("replica") * lax.axis_size("fsdp"))
    summed = lax.psum(shard_rows, "replica").astype(jnp.float32)
    new_master, new_one, new_two = adamw(summed / count, master, moment_one, moment_two)
    return (input_grads, new_master, new_one, new_two)


def exchange(R, T, H, K, lens, acts, grads_in, master, ig_out, grad_out, G, M, W, part, core_in,
             y_in, x_in, l_sem, w_sem, ys, yr, zs, zr, xs, xr, cs, cr, mzs, mzr, mys, myr, igs, igr):
    r, f, t = lax.axis_index("replica"), lax.axis_index("fsdp"), lax.axis_index("tensor")
    x, c = t // 2, t % 2
    other_f, sib, across = 1 - f, 2 * x + 1 - c, 2 * (1 - x) + c
    width = 4 * LANE
    half = H // 2

    def dev(replica=r, fsdp=f, tensor=t):
        return {"replica": replica, "fsdp": fsdp, "tensor": tensor}

    def remote(src, dst, send, recv, to):
        return pltpu.make_async_remote_copy(
            src_ref=src, dst_ref=dst, send_sem=send, recv_sem=recv, device_id=to, device_id_type=MESH
        )

    def rows(o, ff):
        return pl.ds(pl.multiple_of((2 * o + ff) * T, T), T)

    def plane(o):
        return pl.ds(pl.multiple_of(2 * o * T, T), 2 * T)

    def lanes(q):
        return pl.ds(pl.multiple_of(q * LANE, LANE), LANE)

    def columns(ff, k, q):
        return pl.ds(pl.multiple_of(ff * H + k * width + q * LANE, LANE), LANE)

    def own_copy(k, j, q):
        return pltpu.make_async_copy(
            acts.at[:, columns(f, k, q)], G.at[k, rows(r, f), lanes(q)], l_sem.at[k, j]
        )

    def y_copy(k, j, q):
        return remote(
            acts.at[:, columns(other_f, k, q)], G.at[k, rows(r, f), lanes(q)],
            ys.at[k, j], yr.at[k, j], dev(fsdp=other_f),
        )

    def z_copy(k, o, way, to):
        ref = G.at[k, plane(o), lanes(t)]
        return remote(ref, ref, zs.at[k, o, way], zr.at[k, o], dev(replica=to))

    def x_copy(k, o, q):
        ref = G.at[k, plane(o), lanes(q)]
        return remote(ref, ref, xs.at[k, o], xr.at[k, o], dev(tensor=across))

    def c_copy(k, j, q):
        ref = G.at[k, :, lanes(q)]
        return remote(ref, ref, cs.at[k, j], cr.at[k, j], dev(tensor=sib))

    def mz_copy(o, way, to):
        ref = M.at[rows(o, f)]
        return remote(ref, ref, mzs.at[o, way], mzr.at[o], dev(replica=to))

    def my_copy(o, ff):
        ref = M.at[rows(o, ff)]
        return remote(ref, ref, mys.at[o], myr.at[o], dev(fsdp=other_f))

    piece = pl.ds(pl.multiple_of(f * T, T), T)
    other_piece = pl.ds(pl.multiple_of(other_f * T, T), T)
    ig_core = remote(part.at[0], core_in, igs.at[0], igr.at[0], dev(tensor=sib))
    ig_y = remote(part.at[1, other_piece], y_in, igs.at[1], igr.at[1], dev(fsdp=other_f))
    ig_x_own = remote(part.at[1, piece], x_in, igs.at[2], igr.at[2], dev(tensor=across))
    ig_x_relay = remote(y_in, x_in, igs.at[2], igr.at[2], dev(tensor=across))
    on = x == f

    def w_copy(j, cc):
        ref = pl.ds(pl.multiple_of(cc * half, half), half)
        return pltpu.make_async_copy(master.at[ref], W.at[ref], w_sem.at[j])

    w_copy(0, 1 - c).start()
    w_copy(1, c).start()

    def start_own(k):
        own_copy(k, 0, t).start()
        own_copy(k, 1, across).start()

    def start_y(k):
        y_copy(k, 0, t).start()
        y_copy(k, 1, across).start()

    @pl.loop(0, K)
    def _(k):
        start_own(k)

    seqs = lens.shape[0]
    seq = T // seqs
    for j in range(seqs):
        at = lax.broadcasted_iota(jnp.int32, (seq, grads_in.shape[1]), 0)
        value = grads_in[j * seq:(j + 1) * seq, :].astype(jnp.float32)
        value = jnp.where(at < lens[j], value, jnp.zeros_like(value))
        M[pl.ds(pl.multiple_of((2 * r + f) * T + j * seq, seq), seq), :] = value.astype(jnp.bfloat16)

    barrier = pltpu.get_barrier_semaphore()
    for to in (dev(fsdp=other_f), dev(tensor=sib), dev(tensor=across)):
        pl.semaphore_signal(barrier, inc=1, device_id=to, device_id_type=MESH)

    @pl.when(r > 0)
    def _():
        pl.semaphore_signal(barrier, inc=1, device_id=dev(replica=r - 1), device_id_type=MESH)

    @pl.when(r < R - 1)
    def _():
        pl.semaphore_signal(barrier, inc=1, device_id=dev(replica=r + 1), device_id_type=MESH)

    @pl.when(jnp.logical_or(r == 0, r == R - 1))
    def _():
        pl.semaphore_wait(barrier, 4)

    @pl.when(jnp.logical_and(r > 0, r < R - 1))
    def _():
        pl.semaphore_wait(barrier, 5)

    my_copy(r, f).start()
    start_y(0)

    @pl.when(r > 0)
    def _():
        mz_copy(r, 1, r - 1).start()

    @pl.when(r < R - 1)
    def _():
        mz_copy(r, 0, r + 1).start()

    def from_left(d, extra, body):
        @pl.when(jnp.logical_and(r >= d, extra))
        def _():
            body(r - d)

    def from_right(d, extra, body):
        @pl.when(jnp.logical_and(r + d < R, extra))
        def _():
            body(r + d)

    def pass_on(start, way):
        @pl.when(r < R - 1 if way == 0 else r > 0)
        def _():
            start(r + 1 if way == 0 else r - 1)

    def weight_terms(slot, cc):
        @pl.loop(0, half // width)
        def _(i):
            w = W[pl.ds(pl.multiple_of(cc * half + i * width, width), width), :].astype(jnp.bfloat16)
            product = lax.dot_general(
                M[plane(r), :], w, (((1,), (1,)), ((), ())), preferred_element_type=jnp.float32
            )
            part[slot, :, pl.ds(pl.multiple_of(i * width, width), width)] = product.astype(jnp.bfloat16)

    @pl.loop(0, K + R + 1)
    def _(s):
        @pl.when(s + 1 < K)
        def _():
            start_y(s + 1)

        for d in range(R - 1, 0, -1):
            k = s - d
            for side, way in ((from_left, 0), (from_right, 1)):
                def arrived(o, k=k, way=way):
                    z_copy(k, o, way, o).wait_recv()
                    pass_on(lambda to: z_copy(k, o, way, to).start(), way)
                    x_copy(k, o, t).start()

                side(d, jnp.logical_and(k >= 0, k < K), arrived)

                def masked_arrived(o, way=way):
                    mz_copy(o, way, o).wait_recv()
                    pass_on(lambda to: mz_copy(o, way, to).start(), way)
                    my_copy(o, f).start()

                side(d, s == d, masked_arrived)

        @pl.when(s < K)
        def _():
            own_copy(s, 0, t).wait()
            own_copy(s, 1, across).wait()
            for j, q in ((0, t), (1, across)):
                remote(
                    acts.at[:, columns(f, s, q)], G.at[s, rows(r, other_f), lanes(q)],
                    ys.at[s, j], yr.at[s, j], dev(fsdp=other_f),
                ).wait_recv()
            for way in (0, 1):
                pass_on(lambda to, way=way: z_copy(s, r, way, to).start(), way)

        for d in range(R - 1, 0, -1):
            k = s - d - 1
            for side in (from_left, from_right):
                side(d, jnp.logical_and(k >= 0, k < K),
                     lambda o, k=k: x_copy(k, o, across).wait_recv())

        full = s - (R - 1)

        @pl.when(jnp.logical_and(full >= 0, full < K))
        def _():
            c_copy(full, 0, t).start()

        @pl.when(jnp.logical_and(full >= 1, full <= K))
        def _():
            c_copy(full - 1, 1, across).start()

        @pl.when(s == 1)
        def _():
            my_copy(r, other_f).wait_recv()
            w_copy(0, 1 - c).wait()
            weight_terms(0, 1 - c)
            ig_core.start()
            w_copy(1, c).wait()
            weight_terms(1, c)

        @pl.when(s == 2)
        def _():
            ig_core.wait_recv()

            @pl.loop(0, 2 * T // 32)
            def _(i):
                at = pl.ds(pl.multiple_of(i * 32, 32), 32)
                total = part[1, at, :].astype(jnp.float32) + core_in[at, :].astype(jnp.float32)
                part[1, at, :] = total.astype(jnp.bfloat16)

            ig_y.start()

            @pl.when(jnp.logical_not(on))
            def _():
                ig_x_own.start()

        @pl.when(s == 4)
        def _():
            ig_y.wait_recv()

            @pl.when(on)
            def _():
                ig_x_relay.start()

        @pl.when(s == R + 1)
        def _():
            for d in range(1, R):
                for side in (from_left, from_right):
                    side(d, True, lambda o: my_copy(o, other_f).wait_recv())

        done = s - R - 1 + 0

        @pl.when(done >= 0)
        def _():
            c_copy(done, 0, sib).wait_recv()
            c_copy(done, 1, 3 - t).wait_recv()
            product = lax.dot_general(
                G[done], M[...], (((0,), (0,)), ((), ())), preferred_element_type=jnp.float32
            )
            grad_out[pl.ds(pl.multiple_of(done * width, width), width), :] = product.astype(jnp.bfloat16)

    ig_x_own.wait_recv()

    @pl.loop(0, T // 32)
    def _(i):
        at = pl.ds(pl.multiple_of(i * 32, 32), 32)
        mine = part[1, pl.ds(pl.multiple_of(f * T + i * 32, 32), 32), :].astype(jnp.float32)
        near = jnp.where(on, mine, y_in[at, :].astype(jnp.float32))
        ig_out[at, :] = (near + x_in[at, :].astype(jnp.float32)).astype(jnp.bfloat16)

    @pl.loop(0, K)
    def _(k):
        for j in (0, 1):
            y_copy(k, j, t).wait_send()
            c_copy(k, j, t).wait_send()
        for way in (0, 1):
            pass_on(lambda to, way=way: z_copy(k, r, way, to).wait_send(), way)
        for d in range(1, R):
            for side, way in ((from_left, 0), (from_right, 1)):
                def drain(o, way=way):
                    pass_on(lambda to: z_copy(k, o, way, to).wait_send(), way)
                    x_copy(k, o, t).wait_send()

                side(d, True, drain)

    my_copy(r, f).wait_send()
    for way in (0, 1):
        pass_on(lambda to, way=way: mz_copy(r, way, to).wait_send(), way)
    for d in range(1, R):
        for side, way in ((from_left, 0), (from_right, 1)):
            def drain_masked(o, way=way):
                pass_on(lambda to: mz_copy(o, way, to).wait_send(), way)
                my_copy(o, f).wait_send()

            side(d, True, drain_masked)
    ig_core.wait_send()
    ig_y.wait_send()
    ig_x_own.wait_send()


def local_fast(R, activations, value_grads, lengths, master, moment_one, moment_two):
    T, D = activations.shape
    H, V = master.shape
    K = H // (4 * LANE)
    half = H // 2
    dma = pltpu.SemaphoreType.DMA
    input_grads, grad_sum = pl.pallas_call(
        functools.partial(exchange, R, T, H, K),
        out_shape=(
            jax.ShapeDtypeStruct((T, half), jnp.bfloat16),
            jax.ShapeDtypeStruct((H, V), jnp.bfloat16),
        ),
        in_specs=[
            pl.BlockSpec(memory_space=pltpu.SMEM),
            pl.BlockSpec(memory_space=pl.ANY),
            pl.BlockSpec(memory_space=pltpu.VMEM),
            pl.BlockSpec(memory_space=pl.ANY),
        ],
        out_specs=(pl.BlockSpec(memory_space=pltpu.VMEM), pl.BlockSpec(memory_space=pltpu.VMEM)),
        scratch_shapes=[
            pltpu.VMEM((K, 2 * R * T, 4 * LANE), jnp.bfloat16),
            pltpu.VMEM((2 * R * T, V), jnp.bfloat16),
            pltpu.VMEM((H, V), jnp.float32),
            pltpu.VMEM((2, 2 * T, half), jnp.bfloat16),
            pltpu.VMEM((2 * T, half), jnp.bfloat16),
            pltpu.VMEM((T, half), jnp.bfloat16),
            pltpu.VMEM((T, half), jnp.bfloat16),
            dma((K, 2)), dma((2,)),
            dma((K, 2)), dma((K, 2)),
            dma((K, R, 2)), dma((K, R)),
            dma((K, R)), dma((K, R)),
            dma((K, 2)), dma((K, 2)),
            dma((R, 2)), dma((R,)),
            dma((R,)), dma((R,)),
            dma((3,)), dma((3,)),
        ],
        compiler_params=pltpu.CompilerParams(
            collective_id=0, has_side_effects=True, vmem_limit_bytes=32 * 1024 * 1024
        ),
        cost_estimate=pl.CostEstimate(
            flops=2 * 2 * R * T * H * V, bytes_accessed=20 * 1024 * 1024, transcendentals=0
        ),
    )(lengths, activations, value_grads, master)
    count = float(T * lax.axis_size("replica") * lax.axis_size("fsdp"))
    new_master, new_one, new_two = adamw(
        grad_sum.astype(jnp.float32) / count, master, moment_one, moment_two
    )
    return (input_grads, new_master, new_one, new_two)


def solution(mesh):
    in_specs = (
        P(("replica", "fsdp"), None),
        P(("replica", "fsdp"), "tensor"),
        P(("replica", "fsdp")),
        P("fsdp", "tensor"),
        P("fsdp", "tensor"),
        P("fsdp", "tensor"),
    )
    out_specs = (
        P(("replica", "fsdp"), "tensor"),
        P("fsdp", "tensor"),
        P("fsdp", "tensor"),
        P("fsdp", "tensor"),
    )
    shape = mesh.shape
    body = local
    if shape["fsdp"] == 2 and shape["tensor"] == 4 and shape["replica"] == 4:
        body = functools.partial(local_fast, shape["replica"])
    return jax.shard_map(body, mesh=mesh, in_specs=in_specs, out_specs=out_specs, check_vma=False)
```

```python
import functools

import jax
import jax.numpy as jnp
from jax import lax
from jax.experimental import pallas as pl
from jax.experimental.pallas import tpu as pltpu
from jax.sharding import PartitionSpec as P

MESH = pl.DeviceIdType.MESH
LANE = 128

beta_one = 0.9
beta_two = 0.95
learn_rate = 0.001
weight_decay = 0.1
adam_step = 10
epsilon = 1e-08


def adamw(grad, master, moment_one, moment_two):
    first = beta_one * moment_one + (1.0 - beta_one) * grad
    second = beta_two * moment_two + (1.0 - beta_two) * grad * grad
    first_hat = first / (1.0 - beta_one**adam_step)
    second_hat = second / (1.0 - beta_two**adam_step)
    updated = master - learn_rate * (
        first_hat / (jnp.sqrt(second_hat) + epsilon) + weight_decay * master
    )
    return (updated, first, second)


def local(activations, value_grads, lengths, master, moment_one, moment_two):
    tok_rows = activations.shape[0]
    seq_count = lengths.shape[0]
    seq_len = tok_rows // seq_count
    index = jnp.arange(tok_rows, dtype=jnp.int32)
    owner = index // seq_len
    pick = owner[:, None] == jnp.arange(seq_count, dtype=jnp.int32)[None, :]
    limit = jnp.sum(jnp.where(pick, lengths[None, :], 0), axis=1)
    masked = jnp.where((index % seq_len < limit)[:, None], value_grads, jnp.zeros_like(value_grads))
    weight = master.astype(jnp.bfloat16)
    terms = lax.dot_general(
        masked,
        lax.all_gather(weight, "fsdp", axis=0, tiled=True),
        (((1,), (1,)), ((), ())),
        preferred_element_type=jnp.float32,
    )
    input_grads = lax.psum_scatter(
        terms.astype(jnp.bfloat16), "tensor", scatter_dimension=1, tiled=True
    )
    shard_rows = lax.psum_scatter(
        lax.dot_general(
            activations, masked, (((0,), (0,)), ((), ())), preferred_element_type=jnp.float32
        ).astype(jnp.bfloat16),
        "fsdp",
        scatter_dimension=0,
        tiled=True,
    )
    count = float(tok_rows * lax.axis_size("replica") * lax.axis_size("fsdp"))
    summed = lax.psum(shard_rows, "replica").astype(jnp.float32)
    new_master, new_one, new_two = adamw(summed / count, master, moment_one, moment_two)
    return (input_grads, new_master, new_one, new_two)


def exchange(R, T, H, K, lens, acts, grads_in, master, one_in, two_in, ig_out, W, one, two, G, M,
             own_in, product, part, core_in, y_in, x_in, l_sem, w_sem, ys, yr, zs, zr, xs, xr, cs, cr, mzs, mzr, mys, myr, igs, igr):
    r, f, t = lax.axis_index("replica"), lax.axis_index("fsdp"), lax.axis_index("tensor")
    x, c = t // 2, t % 2
    other_f, sib, across = 1 - f, 2 * x + 1 - c, 2 * (1 - x) + c
    width = 4 * LANE
    half = H // 2

    def dev(replica=r, fsdp=f, tensor=t):
        return {"replica": replica, "fsdp": fsdp, "tensor": tensor}

    def remote(src, dst, send, recv, to):
        return pltpu.make_async_remote_copy(
            src_ref=src, dst_ref=dst, send_sem=send, recv_sem=recv, device_id=to, device_id_type=MESH
        )

    def rows(o, ff):
        return pl.ds(pl.multiple_of((2 * o + ff) * T, T), T)

    def plane(o):
        return pl.ds(pl.multiple_of(2 * o * T, T), 2 * T)

    def lanes(q):
        return pl.ds(pl.multiple_of(q * LANE, LANE), LANE)

    def columns(ff, k, q):
        return pl.ds(pl.multiple_of(ff * H + k * width + q * LANE, LANE), LANE)

    def own_copy(k, j, q):
        return pltpu.make_async_copy(
            acts.at[:, columns(f, k, q)], G.at[k, rows(r, f), lanes(q)], l_sem.at[k, j]
        )

    def y_copy(k, j, q):
        return remote(
            acts.at[:, columns(other_f, k, q)], G.at[k, rows(r, f), lanes(q)],
            ys.at[k, j], yr.at[k, j], dev(fsdp=other_f),
        )

    def z_copy(k, o, way, to):
        ref = G.at[k, plane(o), lanes(t)]
        return remote(ref, ref, zs.at[k, o, way], zr.at[k, o], dev(replica=to))

    def x_copy(k, o, q):
        ref = G.at[k, plane(o), lanes(q)]
        return remote(ref, ref, xs.at[k, o], xr.at[k, o], dev(tensor=across))

    def c_copy(k, j, q):
        ref = G.at[k, :, lanes(q)]
        return remote(ref, ref, cs.at[k, j], cr.at[k, j], dev(tensor=sib))

    def mz_copy(o, way, to):
        ref = M.at[rows(o, f)]
        return remote(ref, ref, mzs.at[o, way], mzr.at[o], dev(replica=to))

    def my_copy(o, ff):
        ref = M.at[rows(o, ff)]
        return remote(ref, ref, mys.at[o], myr.at[o], dev(fsdp=other_f))

    piece = pl.ds(pl.multiple_of(f * T, T), T)
    other_piece = pl.ds(pl.multiple_of(other_f * T, T), T)
    ig_core = remote(part.at[0], core_in, igs.at[0], igr.at[0], dev(tensor=sib))
    ig_y = remote(part.at[1, other_piece], y_in, igs.at[1], igr.at[1], dev(fsdp=other_f))
    ig_x_own = remote(part.at[1, piece], x_in, igs.at[2], igr.at[2], dev(tensor=across))
    ig_x_relay = remote(y_in, x_in, igs.at[2], igr.at[2], dev(tensor=across))
    on = x == f

    def w_copy(j, cc):
        ref = pl.ds(pl.multiple_of(cc * half, half), half)
        return pltpu.make_async_copy(master.at[ref], W.at[ref], w_sem.at[j])

    grads_copy = pltpu.make_async_copy(grads_in, own_in, w_sem.at[2])
    one_copy = pltpu.make_async_copy(one_in, one, w_sem.at[3])
    two_copy = pltpu.make_async_copy(two_in, two, w_sem.at[4])
    grads_copy.start()
    w_copy(0, 1 - c).start()

    def start_own(k):
        own_copy(k, 0, t).start()
        own_copy(k, 1, across).start()

    def start_y(k):
        y_copy(k, 0, t).start()
        y_copy(k, 1, across).start()

    @pl.loop(0, K)
    def _(k):
        start_own(k)

    w_copy(1, c).start()
    one_copy.start()
    two_copy.start()
    grads_copy.wait()
    seqs = lens.shape[0]
    seq = T // seqs
    for j in range(seqs):
        at = lax.broadcasted_iota(jnp.int32, (seq, own_in.shape[1]), 0)
        value = own_in[j * seq:(j + 1) * seq, :].astype(jnp.float32)
        value = jnp.where(at < lens[j], value, jnp.zeros_like(value))
        M[pl.ds(pl.multiple_of((2 * r + f) * T + j * seq, seq), seq), :] = value.astype(jnp.bfloat16)

    barrier = pltpu.get_barrier_semaphore()
    for to in (dev(fsdp=other_f), dev(tensor=sib), dev(tensor=across)):
        pl.semaphore_signal(barrier, inc=1, device_id=to, device_id_type=MESH)

    @pl.when(r > 0)
    def _():
        pl.semaphore_signal(barrier, inc=1, device_id=dev(replica=r - 1), device_id_type=MESH)

    @pl.when(r < R - 1)
    def _():
        pl.semaphore_signal(barrier, inc=1, device_id=dev(replica=r + 1), device_id_type=MESH)

    @pl.when(jnp.logical_or(r == 0, r == R - 1))
    def _():
        pl.semaphore_wait(barrier, 4)

    @pl.when(jnp.logical_and(r > 0, r < R - 1))
    def _():
        pl.semaphore_wait(barrier, 5)

    my_copy(r, f).start()
    start_y(0)
    start_y(1)

    @pl.when(r > 0)
    def _():
        mz_copy(r, 1, r - 1).start()

    @pl.when(r < R - 1)
    def _():
        mz_copy(r, 0, r + 1).start()

    def from_left(d, extra, body):
        @pl.when(jnp.logical_and(r >= d, extra))
        def _():
            body(r - d)

    def from_right(d, extra, body):
        @pl.when(jnp.logical_and(r + d < R, extra))
        def _():
            body(r + d)

    def pass_on(start, way):
        @pl.when(r < R - 1 if way == 0 else r > 0)
        def _():
            start(r + 1 if way == 0 else r - 1)

    def weight_terms(slot, cc):
        @pl.loop(0, half // width)
        def _(i):
            w = W[pl.ds(pl.multiple_of(cc * half + i * width, width), width), :].astype(jnp.bfloat16)
            product = lax.dot_general(
                M[plane(r), :], w, (((1,), (1,)), ((), ())), preferred_element_type=jnp.float32
            )
            part[slot, :, pl.ds(pl.multiple_of(i * width, width), width)] = product.astype(jnp.bfloat16)

    @pl.loop(0, K + R + 1)
    def _(s):
        @pl.when(s + 2 < K)
        def _():
            start_y(s + 2)

        @pl.when(s < K)
        def _():
            own_copy(s, 0, t).wait()
            own_copy(s, 1, across).wait()
            for j, q in ((0, t), (1, across)):
                remote(
                    acts.at[:, columns(f, s, q)], G.at[s, rows(r, other_f), lanes(q)],
                    ys.at[s, j], yr.at[s, j], dev(fsdp=other_f),
                ).wait_recv()
            for way in (0, 1):
                pass_on(lambda to, way=way: z_copy(s, r, way, to).start(), way)
        for d in range(R - 1, 0, -1):
            k = s - d
            for side, way in ((from_left, 0), (from_right, 1)):
                def arrived(o, k=k, way=way):
                    z_copy(k, o, way, o).wait_recv()
                    pass_on(lambda to: z_copy(k, o, way, to).start(), way)
                    x_copy(k, o, t).start()

                side(d, jnp.logical_and(k >= 0, k < K), arrived)

                def masked_arrived(o, way=way):
                    mz_copy(o, way, o).wait_recv()
                    pass_on(lambda to: mz_copy(o, way, to).start(), way)
                    my_copy(o, f).start()

                side(d, s == d, masked_arrived)

        for d in range(R - 1, 0, -1):
            k = s - d - 1
            for side in (from_left, from_right):
                side(d, jnp.logical_and(k >= 0, k < K),
                     lambda o, k=k: x_copy(k, o, across).wait_recv())

        full = s - (R - 1)

        @pl.when(jnp.logical_and(full >= 0, full < K))
        def _():
            c_copy(full, 0, t).start()

        @pl.when(jnp.logical_and(full >= 1, full <= K))
        def _():
            c_copy(full - 1, 1, across).start()

        @pl.when(s == 1)
        def _():
            my_copy(r, other_f).wait_recv()
            w_copy(0, 1 - c).wait()
            weight_terms(0, 1 - c)
            ig_core.start()
            w_copy(1, c).wait()
            weight_terms(1, c)

        @pl.when(s == 2)
        def _():
            ig_core.wait_recv()

            @pl.loop(0, 2 * T // 32)
            def _(i):
                at = pl.ds(pl.multiple_of(i * 32, 32), 32)
                total = part[1, at, :].astype(jnp.float32) + core_in[at, :].astype(jnp.float32)
                part[1, at, :] = total.astype(jnp.bfloat16)

            ig_y.start()

            @pl.when(jnp.logical_not(on))
            def _():
                ig_x_own.start()

        @pl.when(s == 4)
        def _():
            ig_y.wait_recv()

            @pl.when(on)
            def _():
                ig_x_relay.start()

        @pl.when(s == R + 1)
        def _():
            for d in range(1, R):
                for side in (from_left, from_right):
                    side(d, True, lambda o: my_copy(o, other_f).wait_recv())

            one_copy.wait()
            two_copy.wait()

        done = s - R - 1

        @pl.when(done >= 0)
        def _():
            c_copy(done, 0, sib).wait_recv()
            c_copy(done, 1, 3 - t).wait_recv()
            product[...] = lax.dot_general(
                G[done], M[...], (((0,), (0,)), ((), ())), preferred_element_type=jnp.float32
            )

            @pl.loop(0, width // 32)
            def _(i):
                at = pl.ds(pl.multiple_of(done * width + i * 32, 32), 32)
                grad = product[pl.ds(pl.multiple_of(i * 32, 32), 32), :] / float(2 * R * T)
                W[at, :], one[at, :], two[at, :] = adamw(grad, W[at, :], one[at, :], two[at, :])

    ig_x_own.wait_recv()

    @pl.loop(0, T // 32)
    def _(i):
        at = pl.ds(pl.multiple_of(i * 32, 32), 32)
        mine = part[1, pl.ds(pl.multiple_of(f * T + i * 32, 32), 32), :].astype(jnp.float32)
        near = jnp.where(on, mine, y_in[at, :].astype(jnp.float32))
        ig_out[at, :] = (near + x_in[at, :].astype(jnp.float32)).astype(jnp.bfloat16)

    @pl.loop(0, K)
    def _(k):
        for j in (0, 1):
            y_copy(k, j, t).wait_send()
            c_copy(k, j, t).wait_send()
        for way in (0, 1):
            pass_on(lambda to, way=way: z_copy(k, r, way, to).wait_send(), way)
        for d in range(1, R):
            for side, way in ((from_left, 0), (from_right, 1)):
                def drain(o, way=way):
                    pass_on(lambda to: z_copy(k, o, way, to).wait_send(), way)
                    x_copy(k, o, t).wait_send()

                side(d, True, drain)

    my_copy(r, f).wait_send()
    for way in (0, 1):
        pass_on(lambda to, way=way: mz_copy(r, way, to).wait_send(), way)
    for d in range(1, R):
        for side, way in ((from_left, 0), (from_right, 1)):
            def drain_masked(o, way=way):
                pass_on(lambda to: mz_copy(o, way, to).wait_send(), way)
                my_copy(o, f).wait_send()

            side(d, True, drain_masked)
    ig_core.wait_send()
    ig_y.wait_send()
    ig_x_own.wait_send()


def write_out(*refs):
    sem = refs[-1]
    half = refs[0].shape[0] // 2
    copies = [
        pltpu.make_async_copy(
            refs[i].at[pl.ds(j * half, half)], refs[3 + i].at[pl.ds(j * half, half)], sem.at[i, j]
        )
        for i in range(3) for j in range(2)
    ]
    for copy in copies:
        copy.start()
    for copy in copies:
        copy.wait()


def local_fast(R, activations, value_grads, lengths, master, moment_one, moment_two):
    T, D = activations.shape
    H, V = master.shape
    K = H // (4 * LANE)
    half = H // 2
    dma = pltpu.SemaphoreType.DMA
    input_grads, *state = pl.pallas_call(
        functools.partial(exchange, R, T, H, K),
        out_shape=(
            jax.ShapeDtypeStruct((T, half), jnp.bfloat16),
        ) + (jax.ShapeDtypeStruct((H, V), jnp.float32),) * 3,
        in_specs=[pl.BlockSpec(memory_space=pltpu.SMEM)] + [pl.BlockSpec(memory_space=pl.ANY)] * 5,
        out_specs=(pl.BlockSpec(memory_space=pltpu.VMEM),) * 4,
        scratch_shapes=[
            pltpu.VMEM((K, 2 * R * T, 4 * LANE), jnp.bfloat16),
            pltpu.VMEM((2 * R * T, V), jnp.bfloat16),
            pltpu.VMEM((T, V), jnp.bfloat16),
            pltpu.VMEM((4 * LANE, V), jnp.float32),
            pltpu.VMEM((2, 2 * T, half), jnp.bfloat16),
            pltpu.VMEM((2 * T, half), jnp.bfloat16),
            pltpu.VMEM((T, half), jnp.bfloat16),
            pltpu.VMEM((T, half), jnp.bfloat16),
            dma((K, 2)), dma((5,)),
            dma((K, 2)), dma((K, 2)),
            dma((K, R, 2)), dma((K, R)),
            dma((K, R)), dma((K, R)),
            dma((K, 2)), dma((K, 2)),
            dma((R, 2)), dma((R,)),
            dma((R,)), dma((R,)),
            dma((3,)), dma((3,)),
        ],
        compiler_params=pltpu.CompilerParams(
            collective_id=0, has_side_effects=True, vmem_limit_bytes=20 * 1024 * 1024
        ),
        cost_estimate=pl.CostEstimate(
            flops=2 * 2 * R * T * H * V, bytes_accessed=60 * 1024 * 1024, transcendentals=0
        ),
    )(lengths, activations, value_grads, master, moment_one, moment_two)
    state = pl.pallas_call(
        write_out,
        out_shape=(jax.ShapeDtypeStruct((H, V), jnp.float32),) * 3,
        in_specs=[pl.BlockSpec(memory_space=pltpu.VMEM)] * 3,
        out_specs=(pl.BlockSpec(memory_space=pl.ANY),) * 3,
        scratch_shapes=[dma((3, 2))],
        compiler_params=pltpu.CompilerParams(vmem_limit_bytes=26 * 1024 * 1024),
    )(*state)
    return (input_grads, *state)


def solution(mesh):
    in_specs = (
        P(("replica", "fsdp"), None),
        P(("replica", "fsdp"), "tensor"),
        P(("replica", "fsdp")),
        P("fsdp", "tensor"),
        P("fsdp", "tensor"),
        P("fsdp", "tensor"),
    )
    out_specs = (
        P(("replica", "fsdp"), "tensor"),
        P("fsdp", "tensor"),
        P("fsdp", "tensor"),
        P("fsdp", "tensor"),
    )
    shape = mesh.shape
    body = local
    if shape["fsdp"] == 2 and shape["tensor"] == 4 and shape["replica"] == 4:
        body = functools.partial(local_fast, shape["replica"])
    return jax.shard_map(body, mesh=mesh, in_specs=in_specs, out_specs=out_specs, check_vma=False)
```

```python
import functools

import jax
import jax.numpy as jnp
from jax import lax
from jax.experimental import pallas as pl
from jax.experimental.pallas import tpu as pltpu
from jax.sharding import PartitionSpec as P

MESH = pl.DeviceIdType.MESH
LANE = 256

beta_one = 0.9
beta_two = 0.95
learn_rate = 0.001
weight_decay = 0.1
adam_step = 10
epsilon = 1e-08


def adamw(grad, master, moment_one, moment_two):
    first = beta_one * moment_one + (1.0 - beta_one) * grad
    second = beta_two * moment_two + (1.0 - beta_two) * grad * grad
    first_hat = first / (1.0 - beta_one**adam_step)
    second_hat = second / (1.0 - beta_two**adam_step)
    updated = master - learn_rate * (
        first_hat / (jnp.sqrt(second_hat) + epsilon) + weight_decay * master
    )
    return (updated, first, second)


def local(activations, value_grads, lengths, master, moment_one, moment_two):
    tok_rows = activations.shape[0]
    seq_count = lengths.shape[0]
    seq_len = tok_rows // seq_count
    index = jnp.arange(tok_rows, dtype=jnp.int32)
    owner = index // seq_len
    pick = owner[:, None] == jnp.arange(seq_count, dtype=jnp.int32)[None, :]
    limit = jnp.sum(jnp.where(pick, lengths[None, :], 0), axis=1)
    masked = jnp.where((index % seq_len < limit)[:, None], value_grads, jnp.zeros_like(value_grads))
    weight = master.astype(jnp.bfloat16)
    terms = lax.dot_general(
        masked,
        lax.all_gather(weight, "fsdp", axis=0, tiled=True),
        (((1,), (1,)), ((), ())),
        preferred_element_type=jnp.float32,
    )
    input_grads = lax.psum_scatter(
        terms.astype(jnp.bfloat16), "tensor", scatter_dimension=1, tiled=True
    )
    shard_rows = lax.psum_scatter(
        lax.dot_general(
            activations, masked, (((0,), (0,)), ((), ())), preferred_element_type=jnp.float32
        ).astype(jnp.bfloat16),
        "fsdp",
        scatter_dimension=0,
        tiled=True,
    )
    count = float(tok_rows * lax.axis_size("replica") * lax.axis_size("fsdp"))
    summed = lax.psum(shard_rows, "replica").astype(jnp.float32)
    new_master, new_one, new_two = adamw(summed / count, master, moment_one, moment_two)
    return (input_grads, new_master, new_one, new_two)


def exchange(R, T, H, K, lens, acts, grads_in, master, one_in, two_in, ig_out, W, one, two, G, M,
             own_in, product, part, core_in, y_in, x_in, l_sem, w_sem, ys, yr, zs, zr, xs, xr, cs, cr, mzs, mzr, mys, myr, igs, igr):
    r, f, t = lax.axis_index("replica"), lax.axis_index("fsdp"), lax.axis_index("tensor")
    x, c = t // 2, t % 2
    other_f, sib, across = 1 - f, 2 * x + 1 - c, 2 * (1 - x) + c
    width = 4 * LANE
    half = H // 2

    def dev(replica=r, fsdp=f, tensor=t):
        return {"replica": replica, "fsdp": fsdp, "tensor": tensor}

    def remote(src, dst, send, recv, to):
        return pltpu.make_async_remote_copy(
            src_ref=src, dst_ref=dst, send_sem=send, recv_sem=recv, device_id=to, device_id_type=MESH
        )

    def rows(o, ff):
        return pl.ds(pl.multiple_of((2 * o + ff) * T, T), T)

    def plane(o):
        return pl.ds(pl.multiple_of(2 * o * T, T), 2 * T)

    def lanes(q):
        return pl.ds(pl.multiple_of(q * LANE, LANE), LANE)

    def columns(ff, k, q):
        return pl.ds(pl.multiple_of(ff * H + k * width + q * LANE, LANE), LANE)

    def own_copy(k, j, q):
        return pltpu.make_async_copy(
            acts.at[:, columns(f, k, q)], G.at[k, rows(r, f), lanes(q)], l_sem.at[k, j]
        )

    def y_copy(k, j, q):
        return remote(
            acts.at[:, columns(other_f, k, q)], G.at[k, rows(r, f), lanes(q)],
            ys.at[k, j], yr.at[k, j], dev(fsdp=other_f),
        )

    def z_copy(k, o, way, to):
        ref = G.at[k, plane(o), lanes(t)]
        return remote(ref, ref, zs.at[k, o, way], zr.at[k, o], dev(replica=to))

    def x_copy(k, o, q):
        ref = G.at[k, plane(o), lanes(q)]
        return remote(ref, ref, xs.at[k, o], xr.at[k, o], dev(tensor=across))

    def c_copy(k, j, q):
        ref = G.at[k, :, lanes(q)]
        return remote(ref, ref, cs.at[k, j], cr.at[k, j], dev(tensor=sib))

    def mz_copy(o, way, to):
        ref = M.at[rows(o, f)]
        return remote(ref, ref, mzs.at[o, way], mzr.at[o], dev(replica=to))

    def my_copy(o, ff):
        ref = M.at[rows(o, ff)]
        return remote(ref, ref, mys.at[o], myr.at[o], dev(fsdp=other_f))

    piece = pl.ds(pl.multiple_of(f * T, T), T)
    other_piece = pl.ds(pl.multiple_of(other_f * T, T), T)
    ig_core = remote(part.at[0], core_in, igs.at[0], igr.at[0], dev(tensor=sib))
    ig_y = remote(part.at[1, other_piece], y_in, igs.at[1], igr.at[1], dev(fsdp=other_f))
    ig_x_own = remote(part.at[1, piece], x_in, igs.at[2], igr.at[2], dev(tensor=across))
    ig_x_relay = remote(y_in, x_in, igs.at[2], igr.at[2], dev(tensor=across))
    on = x == f

    def w_copy(j, cc):
        ref = pl.ds(pl.multiple_of(cc * half, half), half)
        return pltpu.make_async_copy(master.at[ref], W.at[ref], w_sem.at[j])

    grads_copy = pltpu.make_async_copy(grads_in, own_in, w_sem.at[2])
    one_copy = pltpu.make_async_copy(one_in, one, w_sem.at[3])
    two_copy = pltpu.make_async_copy(two_in, two, w_sem.at[4])
    grads_copy.start()
    w_copy(0, 1 - c).start()

    def start_own(k):
        own_copy(k, 0, t).start()
        own_copy(k, 1, across).start()

    def start_y(k):
        y_copy(k, 0, t).start()
        y_copy(k, 1, across).start()

    @pl.loop(0, K)
    def _(k):
        start_own(k)

    w_copy(1, c).start()
    one_copy.start()
    two_copy.start()
    grads_copy.wait()
    seqs = lens.shape[0]
    seq = T // seqs
    for j in range(seqs):
        at = lax.broadcasted_iota(jnp.int32, (seq, own_in.shape[1]), 0)
        value = own_in[j * seq:(j + 1) * seq, :].astype(jnp.float32)
        value = jnp.where(at < lens[j], value, jnp.zeros_like(value))
        M[pl.ds(pl.multiple_of((2 * r + f) * T + j * seq, seq), seq), :] = value.astype(jnp.bfloat16)

    barrier = pltpu.get_barrier_semaphore()
    for to in (dev(fsdp=other_f), dev(tensor=sib), dev(tensor=across)):
        pl.semaphore_signal(barrier, inc=1, device_id=to, device_id_type=MESH)

    @pl.when(r > 0)
    def _():
        pl.semaphore_signal(barrier, inc=1, device_id=dev(replica=r - 1), device_id_type=MESH)

    @pl.when(r < R - 1)
    def _():
        pl.semaphore_signal(barrier, inc=1, device_id=dev(replica=r + 1), device_id_type=MESH)

    @pl.when(jnp.logical_or(r == 0, r == R - 1))
    def _():
        pl.semaphore_wait(barrier, 4)

    @pl.when(jnp.logical_and(r > 0, r < R - 1))
    def _():
        pl.semaphore_wait(barrier, 5)

    my_copy(r, f).start()
    start_y(0)
    start_y(1)

    @pl.when(r > 0)
    def _():
        mz_copy(r, 1, r - 1).start()

    @pl.when(r < R - 1)
    def _():
        mz_copy(r, 0, r + 1).start()

    def from_left(d, extra, body):
        @pl.when(jnp.logical_and(r >= d, extra))
        def _():
            body(r - d)

    def from_right(d, extra, body):
        @pl.when(jnp.logical_and(r + d < R, extra))
        def _():
            body(r + d)

    def pass_on(start, way):
        @pl.when(r < R - 1 if way == 0 else r > 0)
        def _():
            start(r + 1 if way == 0 else r - 1)

    def weight_terms(slot, cc):
        @pl.loop(0, half // width)
        def _(i):
            w = W[pl.ds(pl.multiple_of(cc * half + i * width, width), width), :].astype(jnp.bfloat16)
            product = lax.dot_general(
                M[plane(r), :], w, (((1,), (1,)), ((), ())), preferred_element_type=jnp.float32
            )
            part[slot, :, pl.ds(pl.multiple_of(i * width, width), width)] = product.astype(jnp.bfloat16)

    @pl.loop(0, K + R + 1)
    def _(s):
        @pl.when(s + 2 < K)
        def _():
            start_y(s + 2)

        @pl.when(s < K)
        def _():
            own_copy(s, 0, t).wait()
            own_copy(s, 1, across).wait()
            for j, q in ((0, t), (1, across)):
                remote(
                    acts.at[:, columns(f, s, q)], G.at[s, rows(r, other_f), lanes(q)],
                    ys.at[s, j], yr.at[s, j], dev(fsdp=other_f),
                ).wait_recv()
            for way in (0, 1):
                pass_on(lambda to, way=way: z_copy(s, r, way, to).start(), way)
        for d in range(R - 1, 0, -1):
            k = s - d
            for side, way in ((from_left, 0), (from_right, 1)):
                def arrived(o, k=k, way=way):
                    z_copy(k, o, way, o).wait_recv()
                    x_copy(k, o, t).start()
                    pass_on(lambda to: z_copy(k, o, way, to).start(), way)

                side(d, jnp.logical_and(k >= 0, k < K), arrived)

                def masked_arrived(o, way=way):
                    mz_copy(o, way, o).wait_recv()
                    pass_on(lambda to: mz_copy(o, way, to).start(), way)
                    my_copy(o, f).start()

                side(d, s == d, masked_arrived)

        for d in range(R - 1, 0, -1):
            k = s - d - 1
            for side in (from_left, from_right):
                side(d, jnp.logical_and(k >= 0, k < K),
                     lambda o, k=k: x_copy(k, o, across).wait_recv())

        full = s - (R - 1)

        @pl.when(jnp.logical_and(full >= 0, full < K))
        def _():
            c_copy(full, 0, t).start()

        @pl.when(jnp.logical_and(full >= 1, full <= K))
        def _():
            c_copy(full - 1, 1, across).start()

        @pl.when(s == 1)
        def _():
            my_copy(r, other_f).wait_recv()
            w_copy(0, 1 - c).wait()
            weight_terms(0, 1 - c)
            ig_core.start()
            w_copy(1, c).wait()
            weight_terms(1, c)

        @pl.when(s == 2)
        def _():
            ig_core.wait_recv()

            @pl.loop(0, 2 * T // 32)
            def _(i):
                at = pl.ds(pl.multiple_of(i * 32, 32), 32)
                total = part[1, at, :].astype(jnp.float32) + core_in[at, :].astype(jnp.float32)
                part[1, at, :] = total.astype(jnp.bfloat16)

            ig_y.start()

            @pl.when(jnp.logical_not(on))
            def _():
                ig_x_own.start()

        @pl.when(s == 4)
        def _():
            ig_y.wait_recv()

            @pl.when(on)
            def _():
                ig_x_relay.start()

        @pl.when(s == R + 1)
        def _():
            for d in range(1, R):
                for side in (from_left, from_right):
                    side(d, True, lambda o: my_copy(o, other_f).wait_recv())

            one_copy.wait()
            two_copy.wait()

        done = s - R - 1

        @pl.when(done >= 0)
        def _():
            c_copy(done, 0, sib).wait_recv()
            c_copy(done, 1, 3 - t).wait_recv()
            product[...] = lax.dot_general(
                G[done], M[...], (((0,), (0,)), ((), ())), preferred_element_type=jnp.float32
            )

            @pl.loop(0, width // 32)
            def _(i):
                at = pl.ds(pl.multiple_of(done * width + i * 32, 32), 32)
                grad = product[pl.ds(pl.multiple_of(i * 32, 32), 32), :] / float(2 * R * T)
                W[at, :], one[at, :], two[at, :] = adamw(grad, W[at, :], one[at, :], two[at, :])

    ig_x_own.wait_recv()

    @pl.loop(0, T // 32)
    def _(i):
        at = pl.ds(pl.multiple_of(i * 32, 32), 32)
        mine = part[1, pl.ds(pl.multiple_of(f * T + i * 32, 32), 32), :].astype(jnp.float32)
        near = jnp.where(on, mine, y_in[at, :].astype(jnp.float32))
        ig_out[at, :] = (near + x_in[at, :].astype(jnp.float32)).astype(jnp.bfloat16)

    @pl.loop(0, K)
    def _(k):
        for j in (0, 1):
            y_copy(k, j, t).wait_send()
            c_copy(k, j, t).wait_send()
        for way in (0, 1):
            pass_on(lambda to, way=way: z_copy(k, r, way, to).wait_send(), way)
        for d in range(1, R):
            for side, way in ((from_left, 0), (from_right, 1)):
                def drain(o, way=way):
                    pass_on(lambda to: z_copy(k, o, way, to).wait_send(), way)
                    x_copy(k, o, t).wait_send()

                side(d, True, drain)

    my_copy(r, f).wait_send()
    for way in (0, 1):
        pass_on(lambda to, way=way: mz_copy(r, way, to).wait_send(), way)
    for d in range(1, R):
        for side, way in ((from_left, 0), (from_right, 1)):
            def drain_masked(o, way=way):
                pass_on(lambda to: mz_copy(o, way, to).wait_send(), way)
                my_copy(o, f).wait_send()

            side(d, True, drain_masked)
    ig_core.wait_send()
    ig_y.wait_send()
    ig_x_own.wait_send()


def write_out(*refs):
    sem = refs[-1]
    half = refs[0].shape[0] // 2
    copies = [
        pltpu.make_async_copy(
            refs[i].at[pl.ds(j * half, half)], refs[3 + i].at[pl.ds(j * half, half)], sem.at[i, j]
        )
        for i in range(3) for j in range(2)
    ]
    for copy in copies:
        copy.start()
    for copy in copies:
        copy.wait()


def local_fast(R, activations, value_grads, lengths, master, moment_one, moment_two):
    T, D = activations.shape
    H, V = master.shape
    K = H // (4 * LANE)
    half = H // 2
    dma = pltpu.SemaphoreType.DMA
    input_grads, *state = pl.pallas_call(
        functools.partial(exchange, R, T, H, K),
        out_shape=(
            jax.ShapeDtypeStruct((T, half), jnp.bfloat16),
        ) + (jax.ShapeDtypeStruct((H, V), jnp.float32),) * 3,
        in_specs=[pl.BlockSpec(memory_space=pltpu.SMEM)] + [pl.BlockSpec(memory_space=pl.ANY)] * 5,
        out_specs=(pl.BlockSpec(memory_space=pltpu.VMEM),) * 4,
        scratch_shapes=[
            pltpu.VMEM((K, 2 * R * T, 4 * LANE), jnp.bfloat16),
            pltpu.VMEM((2 * R * T, V), jnp.bfloat16),
            pltpu.VMEM((T, V), jnp.bfloat16),
            pltpu.VMEM((4 * LANE, V), jnp.float32),
            pltpu.VMEM((2, 2 * T, half), jnp.bfloat16),
            pltpu.VMEM((2 * T, half), jnp.bfloat16),
            pltpu.VMEM((T, half), jnp.bfloat16),
            pltpu.VMEM((T, half), jnp.bfloat16),
            dma((K, 2)), dma((5,)),
            dma((K, 2)), dma((K, 2)),
            dma((K, R, 2)), dma((K, R)),
            dma((K, R)), dma((K, R)),
            dma((K, 2)), dma((K, 2)),
            dma((R, 2)), dma((R,)),
            dma((R,)), dma((R,)),
            dma((3,)), dma((3,)),
        ],
        compiler_params=pltpu.CompilerParams(
            collective_id=0, has_side_effects=True, vmem_limit_bytes=20 * 1024 * 1024
        ),
        cost_estimate=pl.CostEstimate(
            flops=2 * 2 * R * T * H * V, bytes_accessed=60 * 1024 * 1024, transcendentals=0
        ),
    )(lengths, activations, value_grads, master, moment_one, moment_two)
    state = pl.pallas_call(
        write_out,
        out_shape=(jax.ShapeDtypeStruct((H, V), jnp.float32),) * 3,
        in_specs=[pl.BlockSpec(memory_space=pltpu.VMEM)] * 3,
        out_specs=(pl.BlockSpec(memory_space=pl.ANY),) * 3,
        scratch_shapes=[dma((3, 2))],
        compiler_params=pltpu.CompilerParams(vmem_limit_bytes=26 * 1024 * 1024),
    )(*state)
    return (input_grads, *state)


def solution(mesh):
    in_specs = (
        P(("replica", "fsdp"), None),
        P(("replica", "fsdp"), "tensor"),
        P(("replica", "fsdp")),
        P("fsdp", "tensor"),
        P("fsdp", "tensor"),
        P("fsdp", "tensor"),
    )
    out_specs = (
        P(("replica", "fsdp"), "tensor"),
        P("fsdp", "tensor"),
        P("fsdp", "tensor"),
        P("fsdp", "tensor"),
    )
    shape = mesh.shape
    body = local
    if shape["fsdp"] == 2 and shape["tensor"] == 4 and shape["replica"] == 4:
        body = functools.partial(local_fast, shape["replica"])
    return jax.shard_map(body, mesh=mesh, in_specs=in_specs, out_specs=out_specs, check_vma=False)
```

```python
import functools

import jax
import jax.numpy as jnp
from jax import lax
from jax.experimental import pallas as pl
from jax.experimental.pallas import tpu as pltpu
from jax.sharding import PartitionSpec as P

MESH = pl.DeviceIdType.MESH
LANE = 256

beta_one = 0.9
beta_two = 0.95
learn_rate = 0.001
weight_decay = 0.1
adam_step = 10
epsilon = 1e-08


def adamw(grad, master, moment_one, moment_two):
    first = beta_one * moment_one + (1.0 - beta_one) * grad
    second = beta_two * moment_two + (1.0 - beta_two) * grad * grad
    first_hat = first / (1.0 - beta_one**adam_step)
    second_hat = second / (1.0 - beta_two**adam_step)
    updated = master - learn_rate * (
        first_hat / (jnp.sqrt(second_hat) + epsilon) + weight_decay * master
    )
    return (updated, first, second)


def local(activations, value_grads, lengths, master, moment_one, moment_two):
    tok_rows = activations.shape[0]
    seq_count = lengths.shape[0]
    seq_len = tok_rows // seq_count
    index = jnp.arange(tok_rows, dtype=jnp.int32)
    owner = index // seq_len
    pick = owner[:, None] == jnp.arange(seq_count, dtype=jnp.int32)[None, :]
    limit = jnp.sum(jnp.where(pick, lengths[None, :], 0), axis=1)
    masked = jnp.where((index % seq_len < limit)[:, None], value_grads, jnp.zeros_like(value_grads))
    weight = master.astype(jnp.bfloat16)
    terms = lax.dot_general(
        masked,
        lax.all_gather(weight, "fsdp", axis=0, tiled=True),
        (((1,), (1,)), ((), ())),
        preferred_element_type=jnp.float32,
    )
    input_grads = lax.psum_scatter(
        terms.astype(jnp.bfloat16), "tensor", scatter_dimension=1, tiled=True
    )
    shard_rows = lax.psum_scatter(
        lax.dot_general(
            activations, masked, (((0,), (0,)), ((), ())), preferred_element_type=jnp.float32
        ).astype(jnp.bfloat16),
        "fsdp",
        scatter_dimension=0,
        tiled=True,
    )
    count = float(tok_rows * lax.axis_size("replica") * lax.axis_size("fsdp"))
    summed = lax.psum(shard_rows, "replica").astype(jnp.float32)
    new_master, new_one, new_two = adamw(summed / count, master, moment_one, moment_two)
    return (input_grads, new_master, new_one, new_two)


def exchange(R, T, H, K, lens, acts, grads_in, master, one_in, two_in, ig_out, W, one, two, G, M,
             own_in, product, part, core_in, y_in, x_in, l_sem, w_sem, ys, yr, zs, zr, xs, xr, cs, cr, mzs, mzr, mys, myr, igs, igr):
    r, f, t = lax.axis_index("replica"), lax.axis_index("fsdp"), lax.axis_index("tensor")
    x, c = t // 2, t % 2
    other_f, sib, across = 1 - f, 2 * x + 1 - c, 2 * (1 - x) + c
    width = 4 * LANE
    half = H // 2

    def dev(replica=r, fsdp=f, tensor=t):
        return {"replica": replica, "fsdp": fsdp, "tensor": tensor}

    def remote(src, dst, send, recv, to):
        return pltpu.make_async_remote_copy(
            src_ref=src, dst_ref=dst, send_sem=send, recv_sem=recv, device_id=to, device_id_type=MESH
        )

    def rows(o, ff):
        return pl.ds(pl.multiple_of((2 * o + ff) * T, T), T)

    def plane(o):
        return pl.ds(pl.multiple_of(2 * o * T, T), 2 * T)

    def lanes(q):
        return pl.ds(pl.multiple_of(q * LANE, LANE), LANE)

    def columns(ff, k, q):
        return pl.ds(pl.multiple_of(ff * H + k * width + q * LANE, LANE), LANE)

    def own_copy(k, j, q):
        return pltpu.make_async_copy(
            acts.at[:, columns(f, k, q)], G.at[k, rows(r, f), lanes(q)], l_sem.at[k, j]
        )

    def y_copy(k, j, q):
        return remote(
            acts.at[:, columns(other_f, k, q)], G.at[k, rows(r, f), lanes(q)],
            ys.at[k, j], yr.at[k, j], dev(fsdp=other_f),
        )

    def z_copy(k, o, way, to):
        ref = G.at[k, plane(o), lanes(t)]
        return remote(ref, ref, zs.at[k, o, way], zr.at[k, o], dev(replica=to))

    def x_copy(k, o, q):
        ref = G.at[k, plane(o), lanes(q)]
        return remote(ref, ref, xs.at[k, o], xr.at[k, o], dev(tensor=across))

    def c_copy(k, j, q):
        ref = G.at[k, :, lanes(q)]
        return remote(ref, ref, cs.at[k, j], cr.at[k, j], dev(tensor=sib))

    def mz_copy(o, way, to):
        ref = M.at[rows(o, f)]
        return remote(ref, ref, mzs.at[o, way], mzr.at[o], dev(replica=to))

    def my_copy(o, ff):
        ref = M.at[rows(o, ff)]
        return remote(ref, ref, mys.at[o], myr.at[o], dev(fsdp=other_f))

    piece = pl.ds(pl.multiple_of(f * T, T), T)
    other_piece = pl.ds(pl.multiple_of(other_f * T, T), T)
    ig_core = remote(part.at[0], core_in, igs.at[0], igr.at[0], dev(tensor=sib))
    ig_y = remote(part.at[1, other_piece], y_in, igs.at[1], igr.at[1], dev(fsdp=other_f))
    ig_x_own = remote(part.at[1, piece], x_in, igs.at[2], igr.at[2], dev(tensor=across))
    ig_x_relay = remote(y_in, x_in, igs.at[2], igr.at[2], dev(tensor=across))
    on = x == f

    def w_copy(j, cc):
        ref = pl.ds(pl.multiple_of(cc * half, half), half)
        return pltpu.make_async_copy(master.at[ref], W.at[ref], w_sem.at[j])

    grads_copy = pltpu.make_async_copy(grads_in, own_in, w_sem.at[2])
    one_copy = pltpu.make_async_copy(one_in, one, w_sem.at[3])
    two_copy = pltpu.make_async_copy(two_in, two, w_sem.at[4])
    grads_copy.start()
    w_copy(0, 1 - c).start()

    def start_own(k):
        own_copy(k, 0, t).start()
        own_copy(k, 1, across).start()

    def start_y(k):
        y_copy(k, 0, t).start()
        y_copy(k, 1, across).start()

    @pl.loop(0, K)
    def _(k):
        start_own(k)

    w_copy(1, c).start()
    one_copy.start()
    two_copy.start()
    grads_copy.wait()
    seqs = lens.shape[0]
    seq = T // seqs
    for j in range(seqs):
        at = lax.broadcasted_iota(jnp.int32, (seq, own_in.shape[1]), 0)
        value = own_in[j * seq:(j + 1) * seq, :].astype(jnp.float32)
        value = jnp.where(at < lens[j], value, jnp.zeros_like(value))
        M[pl.ds(pl.multiple_of((2 * r + f) * T + j * seq, seq), seq), :] = value.astype(jnp.bfloat16)

    barrier = pltpu.get_barrier_semaphore()
    for to in (dev(fsdp=other_f), dev(tensor=sib), dev(tensor=across)):
        pl.semaphore_signal(barrier, inc=1, device_id=to, device_id_type=MESH)

    @pl.when(r > 0)
    def _():
        pl.semaphore_signal(barrier, inc=1, device_id=dev(replica=r - 1), device_id_type=MESH)

    @pl.when(r < R - 1)
    def _():
        pl.semaphore_signal(barrier, inc=1, device_id=dev(replica=r + 1), device_id_type=MESH)

    @pl.when(jnp.logical_or(r == 0, r == R - 1))
    def _():
        pl.semaphore_wait(barrier, 4)

    @pl.when(jnp.logical_and(r > 0, r < R - 1))
    def _():
        pl.semaphore_wait(barrier, 5)

    my_copy(r, f).start()
    start_y(0)
    start_y(1)

    @pl.when(r > 0)
    def _():
        mz_copy(r, 1, r - 1).start()

    @pl.when(r < R - 1)
    def _():
        mz_copy(r, 0, r + 1).start()

    def from_left(d, extra, body):
        @pl.when(jnp.logical_and(r >= d, extra))
        def _():
            body(r - d)

    def from_right(d, extra, body):
        @pl.when(jnp.logical_and(r + d < R, extra))
        def _():
            body(r + d)

    def pass_on(start, way):
        @pl.when(r < R - 1 if way == 0 else r > 0)
        def _():
            start(r + 1 if way == 0 else r - 1)

    def weight_terms(slot, cc):
        @pl.loop(0, half // width)
        def _(i):
            w = W[pl.ds(pl.multiple_of(cc * half + i * width, width), width), :].astype(jnp.bfloat16)
            product = lax.dot_general(
                M[plane(r), :], w, (((1,), (1,)), ((), ())), preferred_element_type=jnp.float32
            )
            part[slot, :, pl.ds(pl.multiple_of(i * width, width), width)] = product.astype(jnp.bfloat16)

    @pl.loop(0, K + R + 1)
    def _(s):
        @pl.when(s + 2 < K)
        def _():
            start_y(s + 2)

        @pl.when(s < K)
        def _():
            own_copy(s, 0, t).wait()
            own_copy(s, 1, across).wait()
            for j, q in ((0, t), (1, across)):
                remote(
                    acts.at[:, columns(f, s, q)], G.at[s, rows(r, other_f), lanes(q)],
                    ys.at[s, j], yr.at[s, j], dev(fsdp=other_f),
                ).wait_recv()
            for way in (0, 1):
                pass_on(lambda to, way=way: z_copy(s, r, way, to).start(), way)
        for d in range(1, R):
            k = s - d
            for side, way in ((from_left, 0), (from_right, 1)):
                def arrived(o, k=k, way=way):
                    z_copy(k, o, way, o).wait_recv()
                    x_copy(k, o, t).start()
                    pass_on(lambda to: z_copy(k, o, way, to).start(), way)

                side(d, jnp.logical_and(k >= 0, k < K), arrived)

                def masked_arrived(o, way=way):
                    mz_copy(o, way, o).wait_recv()
                    pass_on(lambda to: mz_copy(o, way, to).start(), way)
                    my_copy(o, f).start()

                side(d, s == d, masked_arrived)

        for d in range(1, R):
            k = s - d - 1
            for side in (from_left, from_right):
                side(d, jnp.logical_and(k >= 0, k < K),
                     lambda o, k=k: x_copy(k, o, across).wait_recv())

        full = s - (R - 1)

        @pl.when(jnp.logical_and(full >= 0, full < K))
        def _():
            c_copy(full, 0, t).start()

        @pl.when(jnp.logical_and(full >= 1, full <= K))
        def _():
            c_copy(full - 1, 1, across).start()

        @pl.when(s == 1)
        def _():
            my_copy(r, other_f).wait_recv()
            w_copy(0, 1 - c).wait()
            weight_terms(0, 1 - c)
            ig_core.start()
            w_copy(1, c).wait()
            weight_terms(1, c)

        @pl.when(s == 2)
        def _():
            ig_core.wait_recv()

            @pl.loop(0, 2 * T // 32)
            def _(i):
                at = pl.ds(pl.multiple_of(i * 32, 32), 32)
                total = part[1, at, :].astype(jnp.float32) + core_in[at, :].astype(jnp.float32)
                part[1, at, :] = total.astype(jnp.bfloat16)

            ig_y.start()

            @pl.when(jnp.logical_not(on))
            def _():
                ig_x_own.start()

        @pl.when(s == 4)
        def _():
            ig_y.wait_recv()

            @pl.when(on)
            def _():
                ig_x_relay.start()

        @pl.when(s == R + 1)
        def _():
            for d in range(1, R):
                for side in (from_left, from_right):
                    side(d, True, lambda o: my_copy(o, other_f).wait_recv())

            one_copy.wait()
            two_copy.wait()

        done = s - R - 1

        @pl.when(done >= 0)
        def _():
            c_copy(done, 0, sib).wait_recv()
            c_copy(done, 1, 3 - t).wait_recv()
            product[...] = lax.dot_general(
                G[done], M[...], (((0,), (0,)), ((), ())), preferred_element_type=jnp.float32
            )

            @pl.loop(0, width // 32)
            def _(i):
                at = pl.ds(pl.multiple_of(done * width + i * 32, 32), 32)
                grad = product[pl.ds(pl.multiple_of(i * 32, 32), 32), :] / float(2 * R * T)
                W[at, :], one[at, :], two[at, :] = adamw(grad, W[at, :], one[at, :], two[at, :])

    ig_x_own.wait_recv()

    @pl.loop(0, T // 32)
    def _(i):
        at = pl.ds(pl.multiple_of(i * 32, 32), 32)
        mine = part[1, pl.ds(pl.multiple_of(f * T + i * 32, 32), 32), :].astype(jnp.float32)
        near = jnp.where(on, mine, y_in[at, :].astype(jnp.float32))
        ig_out[at, :] = (near + x_in[at, :].astype(jnp.float32)).astype(jnp.bfloat16)

    @pl.loop(0, K)
    def _(k):
        for j in (0, 1):
            y_copy(k, j, t).wait_send()
            c_copy(k, j, t).wait_send()
        for way in (0, 1):
            pass_on(lambda to, way=way: z_copy(k, r, way, to).wait_send(), way)
        for d in range(1, R):
            for side, way in ((from_left, 0), (from_right, 1)):
                def drain(o, way=way):
                    pass_on(lambda to: z_copy(k, o, way, to).wait_send(), way)
                    x_copy(k, o, t).wait_send()

                side(d, True, drain)

    my_copy(r, f).wait_send()
    for way in (0, 1):
        pass_on(lambda to, way=way: mz_copy(r, way, to).wait_send(), way)
    for d in range(1, R):
        for side, way in ((from_left, 0), (from_right, 1)):
            def drain_masked(o, way=way):
                pass_on(lambda to: mz_copy(o, way, to).wait_send(), way)
                my_copy(o, f).wait_send()

            side(d, True, drain_masked)
    ig_core.wait_send()
    ig_y.wait_send()
    ig_x_own.wait_send()


def write_out(*refs):
    sem = refs[-1]
    copies = []
    for i in range(4):
        half = refs[i].shape[0] // 2
        for j in range(2):
            at = pl.ds(j * half, half)
            copies.append(pltpu.make_async_copy(refs[i].at[at], refs[4 + i].at[at], sem.at[i, j]))
    for copy in copies:
        copy.start()
    for copy in copies:
        copy.wait()


def local_fast(R, activations, value_grads, lengths, master, moment_one, moment_two):
    T, D = activations.shape
    H, V = master.shape
    K = H // (4 * LANE)
    half = H // 2
    dma = pltpu.SemaphoreType.DMA
    results = pl.pallas_call(
        functools.partial(exchange, R, T, H, K),
        out_shape=(
            jax.ShapeDtypeStruct((T, half), jnp.bfloat16),
        ) + (jax.ShapeDtypeStruct((H, V), jnp.float32),) * 3,
        in_specs=[pl.BlockSpec(memory_space=pltpu.SMEM)] + [pl.BlockSpec(memory_space=pl.ANY)] * 5,
        out_specs=(pl.BlockSpec(memory_space=pltpu.VMEM),) * 4,
        scratch_shapes=[
            pltpu.VMEM((K, 2 * R * T, 4 * LANE), jnp.bfloat16),
            pltpu.VMEM((2 * R * T, V), jnp.bfloat16),
            pltpu.VMEM((T, V), jnp.bfloat16),
            pltpu.VMEM((4 * LANE, V), jnp.float32),
            pltpu.VMEM((2, 2 * T, half), jnp.bfloat16),
            pltpu.VMEM((2 * T, half), jnp.bfloat16),
            pltpu.VMEM((T, half), jnp.bfloat16),
            pltpu.VMEM((T, half), jnp.bfloat16),
            dma((K, 2)), dma((5,)),
            dma((K, 2)), dma((K, 2)),
            dma((K, R, 2)), dma((K, R)),
            dma((K, R)), dma((K, R)),
            dma((K, 2)), dma((K, 2)),
            dma((R, 2)), dma((R,)),
            dma((R,)), dma((R,)),
            dma((3,)), dma((3,)),
        ],
        compiler_params=pltpu.CompilerParams(
            collective_id=0, has_side_effects=True, vmem_limit_bytes=20 * 1024 * 1024
        ),
        cost_estimate=pl.CostEstimate(
            flops=2 * 2 * R * T * H * V, bytes_accessed=60 * 1024 * 1024, transcendentals=0
        ),
    )(lengths, activations, value_grads, master, moment_one, moment_two)
    return pl.pallas_call(
        write_out,
        out_shape=tuple(jax.ShapeDtypeStruct(v.shape, v.dtype) for v in results),
        in_specs=[pl.BlockSpec(memory_space=pltpu.VMEM)] * 4,
        out_specs=(pl.BlockSpec(memory_space=pl.ANY),) * 4,
        scratch_shapes=[dma((4, 2))],
        compiler_params=pltpu.CompilerParams(vmem_limit_bytes=26 * 1024 * 1024),
    )(*results)


def solution(mesh):
    in_specs = (
        P(("replica", "fsdp"), None),
        P(("replica", "fsdp"), "tensor"),
        P(("replica", "fsdp")),
        P("fsdp", "tensor"),
        P("fsdp", "tensor"),
        P("fsdp", "tensor"),
    )
    out_specs = (
        P(("replica", "fsdp"), "tensor"),
        P("fsdp", "tensor"),
        P("fsdp", "tensor"),
        P("fsdp", "tensor"),
    )
    shape = mesh.shape
    body = local
    if shape["fsdp"] == 2 and shape["tensor"] == 4 and shape["replica"] == 4:
        body = functools.partial(local_fast, shape["replica"])
    return jax.shard_map(body, mesh=mesh, in_specs=in_specs, out_specs=out_specs, check_vma=False)
```
